32 devices in a mesh: group: 2 (over core), kvh: 4 (over z), blk: 4 (over y, x).
Axes of the slice: x: 2, y: 2, z: 4, core: 2. Of those that a mesh axis runs over, the one named last changes fastest.
Arguments:
- resp_q: bfloat16 [1024, 64, 128], P(('group', 'blk'), 'kvh'), parts along dimension 0, may hold values from -8 to 8
- prompt_k: bfloat16 [2048, 8, 128], P(('group', 'blk'), 'kvh'), parts along dimension 0, may hold values from -8 to 8
- prompt_v: bfloat16 [2048, 8, 128], P(('group', 'blk'), 'kvh'), parts along dimension 0, may hold values from -6 to 6
- resp_k: bfloat16 [1024, 8, 128], P(('group', 'blk'), 'kvh'), parts along dimension 0, may hold values from -6 to 6
- resp_v: bfloat16 [1024, 8, 128], P(('group', 'blk'), 'kvh'), parts along dimension 0, may hold values from -6 to 6
- d_out: bfloat16 [1024, 64, 128], P(('group', 'blk'), 'kvh'), parts along dimension 0, may hold values from -6 to 6
- segment_ids: int32 [8, 128], P(('group', 'blk')), parts along dimension 0, may hold values from 0 to 3, never falling along the last dimension, each value on 1 to 64 neighbouring positions
- live_rows: int32 [8], P(('group', 'blk')), parts along dimension 0, may hold values from 1 to 128, 320 in all
Outputs:
- out: bfloat16 [1024, 64, 128], P(('group', 'blk'), 'kvh'), parts along dimension 0
- d_q: bfloat16 [1024, 64, 128], P(('group', 'blk'), 'kvh'), parts along dimension 0
- d_resp_k: bfloat16 [1024, 8, 128], P(('group', 'blk'), 'kvh'), parts along dimension 0
- d_resp_v: bfloat16 [1024, 8, 128], P(('group', 'blk'), 'kvh'), parts along dimension 0
- d_prompt_k: bfloat16 [2048, 8, 128], P(('group', 'blk'), 'kvh'), parts along dimension 0
- d_prompt_v: bfloat16 [2048, 8, 128], P(('group', 'blk'), 'kvh'), parts along dimension 0
The draws below stay inside these ranges and needn't reach their ends.
There are 2 independent parts, one for each index of `group`. The reference program is written for one: setup_inputs(seed, part) draws one part's arguments, and reference() takes and returns one part's arrays. A program takes and returns all parts, laid end to end along the dimension named above; each array names one. Nothing has to cross between parts.
Inputs may be any that keep to these rules, and one draw needn't show every extreme that they name: `segment_ids`: within a device's rows the numbers never fall; one response holds at most 64 rows of a device, and some response reaches that. `live_rows`: rows of a device from this count on are padding; some device has all 128 rows live.
All inputs are finite; a program needn't handle non-finite values.
Results may differ from the reference program's by a relative error of at most 0.017.
Values may be sent and summed in bfloat16 or wider, within the bound.
A program may use at most 64 MiB of HBM per device.

```python
import math
import jax
import jax.numpy as jnp
import numpy as np
from jax import lax

QH = 64
KVH = 8
HD = 128
R_DEV = 128
RESP_DEVS = 4
PROMPT = 1024
RESP = 512


def draw_resp_q(key, part):
    key = jax.random.fold_in(key, 3)
    values = jnp.clip(jax.random.normal(key, (RESP, QH, HD), jnp.float32), -6.0, 6.0)
    return values.astype(jnp.bfloat16)


def draw_prompt_k(key, part):
    key = jax.random.fold_in(key, 5)
    values = jnp.clip(jax.random.normal(key, (PROMPT, KVH, HD), jnp.float32), -6.0, 6.0)
    return values.astype(jnp.bfloat16)


def steps_of(stream_key, extent, pieces, least, high):
    level = 1.0
    for axis_at, blocks in pieces:
        heights = jax.random.uniform(jax.random.fold_in(jax.random.fold_in(stream_key, 6), axis_at), (blocks,), jnp.float32, least / len(pieces), high / len(pieces))
        level = level * jnp.repeat(jnp.exp(heights), extent[axis_at] // blocks).reshape((-1,) + (1,) * (len(extent) - 1 - axis_at))
    return level


def profile(count, total, limit, slope):
    loads = [(1 << 20) // math.isqrt(grade ** slope) + 1 for grade in range(2, count + 1)]
    surplus, holding = total - limit - (count - 1), [1] * (count - 1)
    while surplus > 0:
        free = [i for i in range(count - 1) if holding[i] < limit]
        whole, remaining = sum([loads[i] for i in free]), surplus
        for i in free:
            extra = min(limit - holding[i], max(1, remaining * loads[i] // whole), surplus)
            holding[i] = holding[i] + extra
            surplus = surplus - extra
    return np.array([limit] + holding)


def uneven_parts(key, amount, total, bound, lean):
    if amount == 2:
        one = jax.random.randint(key, (), max(1, total - bound), min(bound, total - 1) + 1)
        return jnp.stack([one, total - one])
    lengths = jnp.asarray(profile(amount, total, bound, lean), jnp.int32)
    couples = (amount - 1) // 2
    giver, taker = lengths[1:1 + 2 * couples:2], lengths[2:2 + 2 * couples:2]
    margin = jnp.minimum(giver - 1, bound - taker)
    moved = jax.random.randint(jax.random.fold_in(key, 1), (couples,), 0, 1 << 20) % (margin + 1)
    lengths = lengths.at[1:1 + 2 * couples:2].set(giver - moved).at[2:2 + 2 * couples:2].set(taker + moved)
    return lengths[jax.random.permutation(jax.random.fold_in(key, 2), amount)]


def noise(rng, shape, width, most, pieces=(), kind=jnp.bfloat16):
    values = jax.random.normal(rng, shape, jnp.float32) * width
    if len(pieces) > 0:
        values = steps_of(rng, shape, pieces, -0.22, 0.18) * values
    return jnp.clip(values, min=-most, max=most).astype(kind)


def setup_inputs(seed: int = 0, part: int = 0) -> dict:
    key_of = jax.random.split(jax.random.key(seed), 9)
    own_keys = jax.random.split(jax.random.fold_in(key_of[8], part), 9)
    return {
        "resp_q": draw_resp_q(jax.random.fold_in(jax.random.fold_in(key_of[8], part), 71), part),
        "prompt_k": draw_prompt_k(jax.random.fold_in(jax.random.fold_in(key_of[8], part), 71), part),
        "prompt_v": noise(own_keys[2], (PROMPT, KVH, HD), 1.0, 6.0, ((0, 4), (1, 4))),
        "resp_k": noise(own_keys[3], (RESP, KVH, HD), 1.0, 6.0, ((0, 4), (1, 4))),
        "resp_v": noise(own_keys[4], (RESP, KVH, HD), 1.0, 6.0, ((0, 4), (1, 4))),
        "d_out": noise(own_keys[5], (RESP, QH, HD), 1.0, 6.0, ((0, 4), (1, 4))),
        "segment_ids": jax.vmap(lambda own: jnp.searchsorted(jnp.cumsum(uneven_parts(own, 4, R_DEV, R_DEV // 2, 2)), jnp.arange(R_DEV), side="right"))(jax.random.split(own_keys[6], RESP_DEVS)).reshape((RESP_DEVS, R_DEV)).astype(jnp.int32),
        "live_rows": uneven_parts(own_keys[7], RESP_DEVS, RESP_DEVS * R_DEV * 5 // 8, R_DEV, 2).astype(jnp.int32),
    }


def round_low(values):
    return lax.optimization_barrier(values.astype(jnp.bfloat16)).astype(jnp.float32)

def reference(resp_q, prompt_k, prompt_v, resp_k, resp_v, d_out, segment_ids, live_rows):
    factor = 1.0 / math.sqrt(HD)
    group_size = QH // KVH
    keys_all = prompt_k.astype(jnp.float32)
    values_all = prompt_v.astype(jnp.float32)
    position = jnp.arange(R_DEV, dtype=jnp.int32)
    highest_precision = lax.Precision.HIGHEST

    def per_device(carry, device):
        grad_k, grad_v = carry
        first_row = (device * R_DEV).astype(jnp.int32)
        query = lax.dynamic_slice_in_dim(resp_q, first_row, R_DEV, 0).astype(jnp.float32).reshape(R_DEV, KVH, group_size, HD)
        own_k = lax.dynamic_slice_in_dim(resp_k, first_row, R_DEV, 0).astype(jnp.float32)
        own_v = lax.dynamic_slice_in_dim(resp_v, first_row, R_DEV, 0).astype(jnp.float32)
        live_count = lax.dynamic_index_in_dim(live_rows, device, 0, keepdims=False)
        segment = lax.dynamic_index_in_dim(segment_ids, device, 0, keepdims=False)
        live_mask = (position < live_count).astype(jnp.float32)
        grad_out = lax.dynamic_slice_in_dim(d_out, first_row, R_DEV, 0).astype(jnp.float32).reshape(R_DEV, KVH, group_size, HD)
        grad_out = grad_out * live_mask[:, None, None, None]
        own_mask = (position[None, :] <= position[:, None]) & (segment[:, None] == segment[None, :])
        prompt_scores = jnp.einsum('rkgd,pkd->kgrp', query, keys_all, precision=highest_precision) * factor
        own_scores = jnp.einsum('rkgd,pkd->kgrp', query, own_k, precision=highest_precision) * factor
        own_scores = jnp.where(own_mask, own_scores, -jnp.inf)
        highest = jnp.maximum(lax.optimization_barrier(jnp.max(prompt_scores, axis=-1)), lax.optimization_barrier(jnp.max(own_scores, axis=-1)))
        exp_total = lax.optimization_barrier(jnp.sum(jnp.exp(prompt_scores - highest[..., None]), axis=-1)) + lax.optimization_barrier(jnp.sum(jnp.exp(own_scores - highest[..., None]), axis=-1))
        log_total = highest + jnp.log(exp_total)
        prompt_full = jnp.exp(prompt_scores - log_total[..., None])
        own_full = jnp.exp(own_scores - log_total[..., None])
        prompt_low = round_low(prompt_full)
        own_low = round_low(own_full)
        accum = jnp.einsum('kgrp,pkd->rkgd', prompt_low, values_all, precision=highest_precision)
        accum = accum + jnp.einsum('kgrp,pkd->rkgd', own_low, own_v, precision=highest_precision)
        out_low = (accum * live_mask[:, None, None, None]).astype(jnp.bfloat16)
        row_delta = jnp.transpose(lax.optimization_barrier(jnp.sum(grad_out * out_low.astype(jnp.float32), axis=-1)), (1, 2, 0))
        prompt_dprob = jnp.einsum('rkgd,pkd->kgrp', grad_out, values_all, precision=highest_precision)
        own_dprob = jnp.einsum('rkgd,pkd->kgrp', grad_out, own_v, precision=highest_precision)
        prompt_dscore = round_low(prompt_full * (prompt_dprob - row_delta[..., None]) * factor)
        own_dscore = round_low(own_full * (own_dprob - row_delta[..., None]) * factor)
        grad_q = jnp.einsum('kgrp,pkd->rkgd', prompt_dscore, keys_all, precision=highest_precision)
        grad_q = grad_q + jnp.einsum('kgrp,pkd->rkgd', own_dscore, own_k, precision=highest_precision)
        grad_k = grad_k + jnp.einsum('kgrp,rkgd->pkd', prompt_dscore, query, precision=highest_precision)
        grad_v = grad_v + jnp.einsum('kgrp,rkgd->pkd', prompt_low, grad_out, precision=highest_precision)
        own_dk = jnp.einsum('kgrp,rkgd->pkd', own_dscore, query, precision=highest_precision)
        own_dv = jnp.einsum('kgrp,rkgd->pkd', own_low, grad_out, precision=highest_precision)
        results = (out_low.reshape(R_DEV, QH, HD), grad_q.astype(jnp.bfloat16).reshape(R_DEV, QH, HD), own_dk.astype(jnp.bfloat16), own_dv.astype(jnp.bfloat16))
        return ((grad_k, grad_v), results)
    zero_grad = jnp.zeros((PROMPT, KVH, HD), jnp.float32)
    sums, stacked = lax.scan(per_device, (zero_grad, zero_grad), jnp.arange(RESP_DEVS, dtype=jnp.int32))
    out = stacked[0].reshape(RESP, QH, HD)
    d_q = stacked[1].reshape(RESP, QH, HD)
    d_resp_k = stacked[2].reshape(RESP, KVH, HD)
    d_resp_v = stacked[3].reshape(RESP, KVH, HD)
    return (out, d_q, d_resp_k, d_resp_v, sums[0].astype(jnp.bfloat16), sums[1].astype(jnp.bfloat16))
```

```python
import functools
import math

import jax
import jax.numpy as jnp
from jax import lax
from jax.experimental import pallas as pl
from jax.experimental.pallas import tpu as pltpu
from jax.sharding import PartitionSpec as P

MESH = pl.DeviceIdType.MESH
BF16 = jnp.bfloat16
F32 = jnp.float32


def mm(a, b):
    return jnp.dot(a, b, preferred_element_type=F32)


def picks(shape, few, many, offset, group):
    one = lax.broadcasted_iota(jnp.int32, shape, few)
    other = lax.broadcasted_iota(jnp.int32, shape, many)
    return (other == group * one + offset).astype(F32).astype(BF16)


def split_heads(merged, group):
    if group == 1:
        return merged
    keys = merged.shape[0] // group
    shape = (keys, group * keys)
    parts = [mm(picks(shape, 0, 1, g, group), merged) for g in range(group)]
    return jnp.concatenate(parts, axis=1).astype(BF16)


def merge_heads(wide, group):
    if group == 1:
        return wide
    keys = wide.shape[0]
    dim = wide.shape[1] // group
    shape = (group * keys, keys)
    parts = [
        mm(picks(shape, 1, 0, g, group), wide[:, g * dim : (g + 1) * dim]) for g in range(group)
    ]
    return sum(parts[1:], parts[0]).astype(BF16)


def kernel(
    n, heads, group,
    live_ref, q_ref, k_ref, v_ref, rk_ref, rv_ref, do_ref, seg_ref,
    out_ref, dq_ref, drk_ref, drv_ref, dpk_ref, dpv_ref,
    kv, q_t, do_t, q_w, do_w, p_all, dp_all, p_loc, dp_loc, w_low, ds_low,
    mask_ref, o_acc, dq_acc, high, low_sum, factor_ref, delta_ref, loc_kv,
    g_out, g_in, send_sem, recv_sem, gsend_sem, grecv_sem,
):
    merged = q_ref.shape[0]
    dim = q_ref.shape[1]
    rows = merged // heads
    keys = k_ref.shape[0] // group
    rkeys = rk_ref.shape[0] // group
    width = 256
    chunks = merged // width
    scale = 1.0 / math.sqrt(dim)
    scale2 = scale * math.log2(math.e)
    me = lax.axis_index("blk")
    pair = n == 4
    if pair:
        xn = me + 1 - 2 * (me % 2)
        yn = (me + 2) % 4
        partners = [xn, yn]
    else:
        partners = [(me + s) % n for s in range(1, n)]

    barrier = pltpu.get_barrier_semaphore()
    for other in partners:
        pl.semaphore_signal(barrier, inc=1, device_id={"blk": other}, device_id_type=MESH)

    kv[0, 0] = split_heads(k_ref[...], group)
    kv[0, 1] = split_heads(v_ref[...], group)
    pl.semaphore_wait(barrier, len(partners))

    def move(src, dst, sem, other):
        return pltpu.make_async_remote_copy(
            src_ref=kv.at[src[0], src[1]], dst_ref=kv.at[dst[0], dst[1]],
            send_sem=send_sem.at[sem], recv_sem=recv_sem.at[sem],
            device_id={"blk": other}, device_id_type=MESH,
        )

    gather = {}
    if pair:
        gather["kx"] = move((0, 0), (1, 0), 0, xn)
        gather["vy"] = move((0, 1), (2, 1), 1, yn)
        gather["vx"] = move((0, 1), (1, 1), 2, xn)
        gather["ky"] = move((0, 0), (2, 0), 3, yn)
        gather["kd"] = move((1, 0), (3, 0), 4, yn)
        gather["vd"] = move((2, 1), (3, 1), 5, xn)
        for name in ("kx", "vy", "vx", "ky"):
            gather[name].start()
    else:
        for s in range(1, n):
            for t in range(2):
                gather[s, t] = move((0, t), (n - s, t), 2 * (n - s) + t, (me + s) % n)
                gather[s, t].start()

    live = live_ref[0]

    def lanes(c):
        return pl.ds(pl.multiple_of(c * width, width), width)

    def prepare(c, carry):
        at = lanes(c)
        row = lax.broadcasted_iota(jnp.int32, (width, dim), 0)
        owner = (row % heads) // (heads // group)
        alive = (row + c * width) // heads < live
        q = q_ref[at, :].astype(F32)
        do = jnp.where(alive, do_ref[at, :].astype(F32), 0.0)
        for value, wide, turned in ((q, q_w, q_t), (do, do_w, do_t)):
            for g in range(group):
                mine = jnp.where(owner == g, value, 0.0)
                span = slice(g * dim, (g + 1) * dim)
                wide[at, span] = mine.astype(BF16)
                turned[span, at] = mine.T.astype(BF16)
        return carry

    lax.fori_loop(0, chunks, prepare, 0)

    def own_head(wide):
        lane = lax.broadcasted_iota(jnp.int32, (dim, width), 1)
        owner = (lane % heads) // (heads // group)
        result = wide[:dim, :]
        for g in range(1, group):
            result = jnp.where(owner == g, wide[g * dim : (g + 1) * dim, :], result)
        return result

    def forward(index, key, value, p_store, dp_store, mask, first):
        value_t = value.astype(F32).T.astype(BF16)

        def step(c, carry):
            at = lanes(c)
            s = mm(key, q_t[:, at])
            if mask is not None:
                s = jnp.where(mask[:, at] > 0.5, s, -1e30)
            top = jnp.max(s, axis=0, keepdims=True)
            p = jnp.exp2((s - top) * scale2)
            p16 = p.astype(BF16)
            p_store[:, at] = p16
            dp_store[:, at] = mm(value, do_t[:, at]).astype(dp_store.dtype)
            o = own_head(mm(value_t, p16))
            total = jnp.sum(p, axis=0, keepdims=True)
            high[index + 1 : index + 2, at] = top
            if first:
                high[0:1, at] = top
                low_sum[0:1, at] = total
                o_acc[:, at] = o
            else:
                old = high[0:1, at]
                new = jnp.maximum(old, top)
                keep = jnp.exp2((old - new) * scale2)
                gain = jnp.exp2((top - new) * scale2)
                high[0:1, at] = new
                low_sum[0:1, at] = low_sum[0:1, at] * keep + total * gain
                o_acc[:, at] = o_acc[:, at] * keep + o * gain
            return carry

        lax.fori_loop(0, chunks, step, 0)

    def forward_slot(s, first=False):
        forward(s, kv[s, 0], kv[s, 1], p_all.at[s], dp_all.at[s], None, first)

    forward_slot(0, True)
    if pair:
        gather["kx"].wait_recv()
        gather["kd"].start()
        gather["vy"].wait_recv()
        gather["vd"].start()

    seg = seg_ref[...].astype(F32)
    ri = lax.broadcasted_iota(jnp.int32, (rkeys, rkeys), 0)
    ci = lax.broadcasted_iota(jnp.int32, (rkeys, rkeys), 1)
    seg_row = jnp.broadcast_to(seg, (rkeys, rkeys))
    seg_col = jnp.sum(jnp.where(ri == ci, seg_row, 0.0), axis=1, keepdims=True)
    allowed = jnp.where((ri <= ci) & (seg_col == seg_row), 1.0, 0.0).astype(BF16)
    er = lax.broadcasted_iota(jnp.int32, (rkeys, merged), 0)
    ec = lax.broadcasted_iota(jnp.int32, (rkeys, merged), 1)
    expand = (er == ec // heads).astype(F32).astype(BF16)
    mask_ref[...] = mm(allowed, expand)
    loc_kv[0] = split_heads(rk_ref[...], group)
    loc_kv[1] = split_heads(rv_ref[...], group)
    forward(n, loc_kv[0], loc_kv[1], p_loc, dp_loc, mask_ref, False)

    if pair:
        gather["vx"].wait_recv()
        forward_slot(1)
        gather["ky"].wait_recv()
        forward_slot(2)
        gather["kd"].wait_recv()
        gather["vd"].wait_recv()
        forward_slot(3)
    else:
        for s in range(n - 1, 0, -1):
            gather[s, 0].wait_recv()
            gather[s, 1].wait_recv()
            forward_slot(n - s)

    def finish(c, carry):
        at = lanes(c)
        inverse = 1.0 / low_sum[0:1, at]
        lane = lax.broadcasted_iota(jnp.int32, (1, width), 1) + c * width
        alive = (lane // heads) < live
        o16 = jnp.where(alive, o_acc[:, at] * inverse, 0.0).astype(BF16)
        o = o16.astype(F32)
        out_ref[at, :] = o.T.astype(BF16)
        do = own_head(do_t[:, at].astype(F32))
        delta_ref[0:1, at] = jnp.sum(do * o, axis=0, keepdims=True)
        top = high[0:1, at]
        for s in range(n + 1):
            factor_ref[s : s + 1, at] = (
                jnp.exp2((high[s + 1 : s + 2, at] - top) * scale2) * inverse
            )
        return carry

    lax.fori_loop(0, chunks, finish, 0)

    def backward(index, key, p_store, dp_store, first):
        key_t = key.astype(F32).T.astype(BF16)
        count = key.shape[0]

        def step(c, carry):
            at = lanes(c)
            w = p_store[:, at].astype(F32) * factor_ref[index : index + 1, at]
            w_low[:count, at] = w.astype(BF16)
            ds = (w * (dp_store[:, at].astype(F32) - delta_ref[0:1, at]) * scale).astype(BF16)
            ds_low[:count, at] = ds
            part = own_head(mm(key_t, ds))
            if first:
                dq_acc[:, at] = part
            else:
                dq_acc[:, at] += part
            return carry

        lax.fori_loop(0, chunks, step, 0)
        return mm(ds_low[:count, :], q_w[...]), mm(w_low[:count, :], do_w[...])

    def backward_slot(s, first=False):
        return backward(s, kv[s, 0], p_all.at[s], dp_all.at[s], first)

    def give(slot, other):
        return pltpu.make_async_remote_copy(
            src_ref=g_out.at[slot], dst_ref=g_in.at[slot],
            send_sem=gsend_sem.at[slot], recv_sem=grecv_sem.at[slot],
            device_id={"blk": other}, device_id_type=MESH,
        )

    back = []
    if pair:
        gk, gv = backward_slot(3, True)
        g_out[0] = gk.astype(BF16)
        kd = give(0, xn)
        kd.start()
        g_out[1] = gv.astype(BF16)
        vd = give(1, yn)
        vd.start()
        gk, gv = backward_slot(1)
        g_out[2] = gk.astype(BF16)
        kx = give(2, xn)
        kx.start()
        vd.wait_recv()
        g_out[3] = (gv + g_in[1].astype(F32)).astype(BF16)
        vx = give(3, xn)
        vx.start()
        gk, gv = backward_slot(2)
        g_out[4] = gv.astype(BF16)
        vy = give(4, yn)
        vy.start()
        kd.wait_recv()
        g_out[5] = (gk + g_in[0].astype(F32)).astype(BF16)
        ky = give(5, yn)
        ky.start()
        back = [kd, vd, kx, vx, vy, ky]
    else:
        for s in range(1, n):
            gk, gv = backward_slot(s, s == 1)
            g_out[2 * s] = gk.astype(BF16)
            g_out[2 * s + 1] = gv.astype(BF16)
            for t in range(2):
                back.append(give(2 * s + t, (me + s) % n))
                back[-1].start()

    gk, gv = backward(n, loc_kv[0], p_loc, dp_loc, False)
    drk_ref[...] = merge_heads(gk.astype(BF16), group)
    drv_ref[...] = merge_heads(gv.astype(BF16), group)
    gk, gv = backward_slot(0)

    def last(c, carry):
        at = lanes(c)
        dq_ref[at, :] = dq_acc[:, at].T.astype(BF16)
        return carry

    lax.fori_loop(0, chunks, last, 0)

    if pair:
        kx.wait_recv()
        vy.wait_recv()
        vx.wait_recv()
        ky.wait_recv()
        gk = gk + g_in[2].astype(F32) + g_in[5].astype(F32)
        gv = gv + g_in[4].astype(F32) + g_in[3].astype(F32)
    else:
        for s in range(1, n):
            back[2 * s - 2].wait_recv()
            back[2 * s - 1].wait_recv()
            gk = gk + g_in[2 * s].astype(F32)
            gv = gv + g_in[2 * s + 1].astype(F32)
    dpk_ref[...] = merge_heads(gk.astype(BF16), group)
    dpv_ref[...] = merge_heads(gv.astype(BF16), group)
    for copy in list(gather.values()) + back:
        copy.wait_send()


def on_device(n, resp_q, prompt_k, prompt_v, resp_k, resp_v, d_out, segment_ids, live_rows):
    rows, heads, dim = resp_q.shape
    keys, kvh, _ = prompt_k.shape
    rkeys = resp_k.shape[0]
    merged = rows * heads
    flat = lambda a: a.reshape(-1, dim)
    vmem = pl.BlockSpec(memory_space=pltpu.VMEM)
    dp_type = F32 if n <= 4 else BF16
    stats = ((n + 2 + 7) // 8) * 8
    grads = 6 if n == 4 else 2 * n
    results = pl.pallas_call(
        functools.partial(kernel, n, heads, kvh),
        out_shape=[
            jax.ShapeDtypeStruct((merged, dim), BF16),
            jax.ShapeDtypeStruct((merged, dim), BF16),
            jax.ShapeDtypeStruct((rkeys * kvh, dim), BF16),
            jax.ShapeDtypeStruct((rkeys * kvh, dim), BF16),
            jax.ShapeDtypeStruct((keys * kvh, dim), BF16),
            jax.ShapeDtypeStruct((keys * kvh, dim), BF16),
        ],
        in_specs=[pl.BlockSpec(memory_space=pltpu.SMEM)] + [vmem] * 7,
        out_specs=[vmem] * 6,
        scratch_shapes=[
            pltpu.VMEM((n, 2, keys, kvh * dim), BF16),
            pltpu.VMEM((kvh * dim, merged), BF16),
            pltpu.VMEM((kvh * dim, merged), BF16),
            pltpu.VMEM((merged, kvh * dim), BF16),
            pltpu.VMEM((merged, kvh * dim), BF16),
            pltpu.VMEM((n, keys, merged), BF16),
            pltpu.VMEM((n, keys, merged), dp_type),
            pltpu.VMEM((rkeys, merged), BF16),
            pltpu.VMEM((rkeys, merged), dp_type),
            pltpu.VMEM((keys, merged), BF16),
            pltpu.VMEM((keys, merged), BF16),
            pltpu.VMEM((rkeys, merged), F32),
            pltpu.VMEM((dim, merged), F32),
            pltpu.VMEM((dim, merged), F32),
            pltpu.VMEM((stats, merged), F32),
            pltpu.VMEM((8, merged), F32),
            pltpu.VMEM((stats, merged), F32),
            pltpu.VMEM((8, merged), F32),
            pltpu.VMEM((2, rkeys, kvh * dim), BF16),
            pltpu.VMEM((grads, keys, kvh * dim), BF16),
            pltpu.VMEM((grads, keys, kvh * dim), BF16),
            pltpu.SemaphoreType.DMA((2 * n,)),
            pltpu.SemaphoreType.DMA((2 * n,)),
            pltpu.SemaphoreType.DMA((grads,)),
            pltpu.SemaphoreType.DMA((grads,)),
        ],
        compiler_params=pltpu.CompilerParams(
            collective_id=0, has_side_effects=True, vmem_limit_bytes=60 * 1024 * 1024
        ),
        cost_estimate=pl.CostEstimate(
            flops=12 * merged * dim * (n * keys + rkeys),
            bytes_accessed=4 * merged * dim * 2,
            transcendentals=merged * (n * keys + rkeys),
        ),
    )(
        live_rows, flat(resp_q), flat(prompt_k), flat(prompt_v), flat(resp_k), flat(resp_v),
        flat(d_out), segment_ids,
    )
    shapes = (resp_q, resp_q, resp_k, resp_v, prompt_k, prompt_v)
    return tuple(r.reshape(s.shape) for r, s in zip(results, shapes))


def solution(mesh):
    split = P(("group", "blk"), "kvh", None)
    return jax.shard_map(
        functools.partial(on_device, mesh.shape["blk"]),
        mesh=mesh,
        in_specs=(split,) * 6 + (P(("group", "blk"), None), P(("group", "blk"))),
        out_specs=(split,) * 6,
        check_vma=False,
    )
```

```python
import functools
import math

import jax
import jax.numpy as jnp
from jax import lax
from jax.experimental import pallas as pl
from jax.experimental.pallas import tpu as pltpu
from jax.sharding import PartitionSpec as P

MESH = pl.DeviceIdType.MESH
BF16 = jnp.bfloat16
F32 = jnp.float32
FWD_UNROLL = 8
BWD_UNROLL = 8
PREP_UNROLL = 2


def mm(a, b):
    return jnp.dot(a, b, preferred_element_type=F32)


def picks(shape, few, many, offset, group):
    one = lax.broadcasted_iota(jnp.int32, shape, few)
    other = lax.broadcasted_iota(jnp.int32, shape, many)
    return (other == group * one + offset).astype(F32).astype(BF16)


def split_heads(merged, group):
    if group == 1:
        return merged
    keys = merged.shape[0] // group
    shape = (keys, group * keys)
    parts = [mm(picks(shape, 0, 1, g, group), merged) for g in range(group)]
    return jnp.concatenate(parts, axis=1).astype(BF16)


def merge_heads(wide, group):
    if group == 1:
        return wide
    keys = wide.shape[0]
    dim = wide.shape[1] // group
    shape = (group * keys, keys)
    parts = [
        mm(picks(shape, 1, 0, g, group), wide[:, g * dim : (g + 1) * dim]) for g in range(group)
    ]
    return sum(parts[1:], parts[0]).astype(BF16)


def kernel(
    n, heads, group,
    live_ref, q_ref, k_ref, v_ref, rk_ref, rv_ref, do_ref, seg_ref,
    out_ref, dq_ref, drk_ref, drv_ref, dpk_ref, dpv_ref,
    kv, q_t, do_t, q_w, do_w, p_all, dp_all, p_loc, dp_loc, w_low, ds_low,
    mask_ref, o_acc, dq_acc, high, low_sum, factor_ref, delta_ref, loc_kv,
    g_out, g_in, send_sem, recv_sem, gsend_sem, grecv_sem,
):
    merged = q_ref.shape[0]
    dim = q_ref.shape[1]
    rows = merged // heads
    keys = k_ref.shape[0] // group
    rkeys = rk_ref.shape[0] // group
    width = 256
    chunks = merged // width
    scale = 1.0 / math.sqrt(dim)
    scale2 = scale * math.log2(math.e)
    me = lax.axis_index("blk")
    pair = n == 4
    if pair:
        xn = me + 1 - 2 * (me % 2)
        yn = (me + 2) % 4
        partners = [xn, yn]
    else:
        partners = [(me + s) % n for s in range(1, n)]

    barrier = pltpu.get_barrier_semaphore()
    for other in partners:
        pl.semaphore_signal(barrier, inc=1, device_id={"blk": other}, device_id_type=MESH)

    kv[0, 0] = split_heads(k_ref[...], group)
    kv[0, 1] = split_heads(v_ref[...], group)
    pl.semaphore_wait(barrier, len(partners))

    def move(src, dst, sem, other):
        return pltpu.make_async_remote_copy(
            src_ref=kv.at[src[0], src[1]], dst_ref=kv.at[dst[0], dst[1]],
            send_sem=send_sem.at[sem], recv_sem=recv_sem.at[sem],
            device_id={"blk": other}, device_id_type=MESH,
        )

    gather = {}
    if pair:
        gather["kx"] = move((0, 0), (1, 0), 0, xn)
        gather["vy"] = move((0, 1), (2, 1), 1, yn)
        gather["vx"] = move((0, 1), (1, 1), 2, xn)
        gather["ky"] = move((0, 0), (2, 0), 3, yn)
        gather["kd"] = move((1, 0), (3, 0), 4, yn)
        gather["vd"] = move((2, 1), (3, 1), 5, xn)
        for name in ("kx", "vy", "vx", "ky"):
            gather[name].start()
    else:
        for s in range(1, n):
            for t in range(2):
                gather[s, t] = move((0, t), (n - s, t), 2 * (n - s) + t, (me + s) % n)
                gather[s, t].start()

    live = live_ref[0]

    def lanes(c):
        return pl.ds(pl.multiple_of(c * width, width), width)

    def prepare(c, carry):
        at = lanes(c)
        row = lax.broadcasted_iota(jnp.int32, (width, dim), 0)
        owner = (row % heads) // (heads // group)
        alive = (row + c * width) // heads < live
        q = q_ref[at, :].astype(F32)
        do = jnp.where(alive, do_ref[at, :].astype(F32), 0.0)
        for value, wide, turned in ((q, q_w, q_t), (do, do_w, do_t)):
            for g in range(group):
                mine = jnp.where(owner == g, value, 0.0)
                span = slice(g * dim, (g + 1) * dim)
                wide[at, span] = mine.astype(BF16)
                turned[span, at] = mine.T.astype(BF16)
        return carry

    lax.fori_loop(0, chunks, prepare, 0, unroll=PREP_UNROLL)

    def own_head(wide):
        lane = lax.broadcasted_iota(jnp.int32, (dim, width), 1)
        owner = (lane % heads) // (heads // group)
        result = wide[:dim, :]
        for g in range(1, group):
            result = jnp.where(owner == g, wide[g * dim : (g + 1) * dim, :], result)
        return result

    def forward(index, key, value, p_store, dp_store, mask, first):
        value_t = value.astype(F32).T.astype(BF16)

        def step(c, carry):
            at = lanes(c)
            s = mm(key, q_t[:, at])
            if mask is not None:
                s = jnp.where(mask[:, at] > 0.5, s, -1e30)
            top = jnp.max(s, axis=0, keepdims=True)
            p = jnp.exp2((s - top) * scale2)
            p16 = p.astype(BF16)
            p_store[:, at] = p16
            dp_store[:, at] = mm(value, do_t[:, at]).astype(dp_store.dtype)
            o = own_head(mm(value_t, p16))
            total = jnp.sum(p, axis=0, keepdims=True)
            high[index + 1 : index + 2, at] = top
            if first:
                high[0:1, at] = top
                low_sum[0:1, at] = total
                o_acc[:, at] = o
            else:
                old = high[0:1, at]
                new = jnp.maximum(old, top)
                keep = jnp.exp2((old - new) * scale2)
                gain = jnp.exp2((top - new) * scale2)
                high[0:1, at] = new
                low_sum[0:1, at] = low_sum[0:1, at] * keep + total * gain
                o_acc[:, at] = o_acc[:, at] * keep + o * gain
            return carry

        lax.fori_loop(0, chunks, step, 0, unroll=FWD_UNROLL)

    def forward_slot(s, first=False):
        forward(s, kv[s, 0], kv[s, 1], p_all.at[s], dp_all.at[s], None, first)

    forward_slot(0, True)
    if pair:
        gather["kx"].wait_recv()
        gather["kd"].start()
        gather["vy"].wait_recv()
        gather["vd"].start()

    seg = seg_ref[...].astype(F32)
    ri = lax.broadcasted_iota(jnp.int32, (rkeys, rkeys), 0)
    ci = lax.broadcasted_iota(jnp.int32, (rkeys, rkeys), 1)
    seg_row = jnp.broadcast_to(seg, (rkeys, rkeys))
    seg_col = jnp.sum(jnp.where(ri == ci, seg_row, 0.0), axis=1, keepdims=True)
    allowed = jnp.where((ri <= ci) & (seg_col == seg_row), 1.0, 0.0).astype(BF16)
    er = lax.broadcasted_iota(jnp.int32, (rkeys, merged), 0)
    ec = lax.broadcasted_iota(jnp.int32, (rkeys, merged), 1)
    expand = (er == ec // heads).astype(F32).astype(BF16)
    mask_ref[...] = mm(allowed, expand)
    loc_kv[0] = split_heads(rk_ref[...], group)
    loc_kv[1] = split_heads(rv_ref[...], group)
    forward(n, loc_kv[0], loc_kv[1], p_loc, dp_loc, mask_ref, False)

    if pair:
        gather["vx"].wait_recv()
        forward_slot(1)
        gather["ky"].wait_recv()
        forward_slot(2)
        gather["kd"].wait_recv()
        gather["vd"].wait_recv()
        forward_slot(3)
    else:
        for s in range(n - 1, 0, -1):
            gather[s, 0].wait_recv()
            gather[s, 1].wait_recv()
            forward_slot(n - s)

    def finish(c, carry):
        at = lanes(c)
        inverse = 1.0 / low_sum[0:1, at]
        lane = lax.broadcasted_iota(jnp.int32, (1, width), 1) + c * width
        alive = (lane // heads) < live
        o16 = jnp.where(alive, o_acc[:, at] * inverse, 0.0).astype(BF16)
        o = o16.astype(F32)
        out_ref[at, :] = o.T.astype(BF16)
        do = own_head(do_t[:, at].astype(F32))
        delta_ref[0:1, at] = jnp.sum(do * o, axis=0, keepdims=True)
        top = high[0:1, at]
        for s in range(n + 1):
            factor_ref[s : s + 1, at] = (
                jnp.exp2((high[s + 1 : s + 2, at] - top) * scale2) * inverse
            )
        return carry

    lax.fori_loop(0, chunks, finish, 0, unroll=PREP_UNROLL)

    def backward(index, key, p_store, dp_store, first):
        key_t = key.astype(F32).T.astype(BF16)
        count = key.shape[0]

        def step(c, carry):
            at = lanes(c)
            w = p_store[:, at].astype(F32) * factor_ref[index : index + 1, at]
            w_low[:count, at] = w.astype(BF16)
            ds = (w * (dp_store[:, at].astype(F32) - delta_ref[0:1, at]) * scale).astype(BF16)
            ds_low[:count, at] = ds
            part = own_head(mm(key_t, ds))
            if first:
                dq_acc[:, at] = part
            else:
                dq_acc[:, at] += part
            return carry

        lax.fori_loop(0, chunks, step, 0, unroll=BWD_UNROLL)
        return mm(ds_low[:count, :], q_w[...]), mm(w_low[:count, :], do_w[...])

    def backward_slot(s, first=False):
        return backward(s, kv[s, 0], p_all.at[s], dp_all.at[s], first)

    def give(slot, other):
        return pltpu.make_async_remote_copy(
            src_ref=g_out.at[slot], dst_ref=g_in.at[slot],
            send_sem=gsend_sem.at[slot], recv_sem=grecv_sem.at[slot],
            device_id={"blk": other}, device_id_type=MESH,
        )

    back = []
    if pair:
        gk, gv = backward_slot(3, True)
        g_out[0] = gk.astype(BF16)
        kd = give(0, xn)
        kd.start()
        g_out[1] = gv.astype(BF16)
        vd = give(1, yn)
        vd.start()
        gk, gv = backward_slot(1)
        g_out[2] = gk.astype(BF16)
        kx = give(2, xn)
        kx.start()
        vd.wait_recv()
        g_out[3] = (gv + g_in[1].astype(F32)).astype(BF16)
        vx = give(3, xn)
        vx.start()
        gk, gv = backward_slot(2)
        g_out[4] = gv.astype(BF16)
        vy = give(4, yn)
        vy.start()
        kd.wait_recv()
        g_out[5] = (gk + g_in[0].astype(F32)).astype(BF16)
        ky = give(5, yn)
        ky.start()
        back = [kd, vd, kx, vx, vy, ky]
    else:
        for s in range(1, n):
            gk, gv = backward_slot(s, s == 1)
            g_out[2 * s] = gk.astype(BF16)
            g_out[2 * s + 1] = gv.astype(BF16)
            for t in range(2):
                back.append(give(2 * s + t, (me + s) % n))
                back[-1].start()

    gk, gv = backward(n, loc_kv[0], p_loc, dp_loc, False)
    drk_ref[...] = merge_heads(gk.astype(BF16), group)
    drv_ref[...] = merge_heads(gv.astype(BF16), group)
    gk, gv = backward_slot(0)

    def last(c, carry):
        at = lanes(c)
        dq_ref[at, :] = dq_acc[:, at].T.astype(BF16)
        return carry

    lax.fori_loop(0, chunks, last, 0, unroll=PREP_UNROLL)

    if pair:
        kx.wait_recv()
        vy.wait_recv()
        vx.wait_recv()
        ky.wait_recv()
        gk = gk + g_in[2].astype(F32) + g_in[5].astype(F32)
        gv = gv + g_in[4].astype(F32) + g_in[3].astype(F32)
    else:
        for s in range(1, n):
            back[2 * s - 2].wait_recv()
            back[2 * s - 1].wait_recv()
            gk = gk + g_in[2 * s].astype(F32)
            gv = gv + g_in[2 * s + 1].astype(F32)
    dpk_ref[...] = merge_heads(gk.astype(BF16), group)
    dpv_ref[...] = merge_heads(gv.astype(BF16), group)
    for copy in list(gather.values()) + back:
        copy.wait_send()


def store_kernel(*refs):
    count = len(refs) // 2
    for i in range(count):
        refs[count + i][...] = refs[i][...]


def store(results):
    vmem = pl.BlockSpec(memory_space=pltpu.VMEM)
    return pl.pallas_call(
        store_kernel,
        out_shape=[jax.ShapeDtypeStruct(r.shape, r.dtype) for r in results],
        in_specs=[vmem] * len(results),
        out_specs=[vmem] * len(results),
    )(*results)


def on_device(n, resp_q, prompt_k, prompt_v, resp_k, resp_v, d_out, segment_ids, live_rows):
    rows, heads, dim = resp_q.shape
    keys, kvh, _ = prompt_k.shape
    rkeys = resp_k.shape[0]
    merged = rows * heads
    flat = lambda a: a.reshape(-1, dim)
    vmem = pl.BlockSpec(memory_space=pltpu.VMEM)
    dp_type = F32 if n <= 4 else BF16
    stats = ((n + 2 + 7) // 8) * 8
    grads = 6 if n == 4 else 2 * n
    results = pl.pallas_call(
        functools.partial(kernel, n, heads, kvh),
        out_shape=[
            jax.ShapeDtypeStruct((merged, dim), BF16),
            jax.ShapeDtypeStruct((merged, dim), BF16),
            jax.ShapeDtypeStruct((rkeys * kvh, dim), BF16),
            jax.ShapeDtypeStruct((rkeys * kvh, dim), BF16),
            jax.ShapeDtypeStruct((keys * kvh, dim), BF16),
            jax.ShapeDtypeStruct((keys * kvh, dim), BF16),
        ],
        in_specs=[pl.BlockSpec(memory_space=pltpu.SMEM)] + [vmem] * 7,
        out_specs=[vmem] * 6,
        scratch_shapes=[
            pltpu.VMEM((n, 2, keys, kvh * dim), BF16),
            pltpu.VMEM((kvh * dim, merged), BF16),
            pltpu.VMEM((kvh * dim, merged), BF16),
            pltpu.VMEM((merged, kvh * dim), BF16),
            pltpu.VMEM((merged, kvh * dim), BF16),
            pltpu.VMEM((n, keys, merged), BF16),
            pltpu.VMEM((n, keys, merged), dp_type),
            pltpu.VMEM((rkeys, merged), BF16),
            pltpu.VMEM((rkeys, merged), dp_type),
            pltpu.VMEM((keys, merged), BF16),
            pltpu.VMEM((keys, merged), BF16),
            pltpu.VMEM((rkeys, merged), F32),
            pltpu.VMEM((dim, merged), F32),
            pltpu.VMEM((dim, merged), F32),
            pltpu.VMEM((stats, merged), F32),
            pltpu.VMEM((8, merged), F32),
            pltpu.VMEM((stats, merged), F32),
            pltpu.VMEM((8, merged), F32),
            pltpu.VMEM((2, rkeys, kvh * dim), BF16),
            pltpu.VMEM((grads, keys, kvh * dim), BF16),
            pltpu.VMEM((grads, keys, kvh * dim), BF16),
            pltpu.SemaphoreType.DMA((2 * n,)),
            pltpu.SemaphoreType.DMA((2 * n,)),
            pltpu.SemaphoreType.DMA((grads,)),
            pltpu.SemaphoreType.DMA((grads,)),
        ],
        compiler_params=pltpu.CompilerParams(
            collective_id=0, has_side_effects=True, vmem_limit_bytes=60 * 1024 * 1024
        ),
        cost_estimate=pl.CostEstimate(
            flops=12 * merged * dim * (n * keys + rkeys),
            bytes_accessed=4 * merged * dim * 2,
            transcendentals=merged * (n * keys + rkeys),
        ),
    )(
        live_rows, flat(resp_q), flat(prompt_k), flat(prompt_v), flat(resp_k), flat(resp_v),
        flat(d_out), segment_ids,
    )
    results = store(results)
    shapes = (resp_q, resp_q, resp_k, resp_v, prompt_k, prompt_v)
    return tuple(r.reshape(s.shape) for r, s in zip(results, shapes))


def solution(mesh):
    split = P(("group", "blk"), "kvh", None)
    return jax.shard_map(
        functools.partial(on_device, mesh.shape["blk"]),
        mesh=mesh,
        in_specs=(split,) * 6 + (P(("group", "blk"), None), P(("group", "blk"))),
        out_specs=(split,) * 6,
        check_vma=False,
    )
```

```python
import functools
import math

import jax
import jax.numpy as jnp
from jax import lax
from jax.experimental import pallas as pl
from jax.experimental.pallas import tpu as pltpu
from jax.sharding import PartitionSpec as P

MESH = pl.DeviceIdType.MESH
BF16 = jnp.bfloat16
F32 = jnp.float32
UNROLL = 8
PREP_UNROLL = 2


def mm(a, b):
    return jnp.dot(a, b, preferred_element_type=F32)


def picks(shape, few, many, offset, group):
    one = lax.broadcasted_iota(jnp.int32, shape, few)
    other = lax.broadcasted_iota(jnp.int32, shape, many)
    return (other == group * one + offset).astype(F32).astype(BF16)


def split_heads(merged, group):
    if group == 1:
        return merged
    keys = merged.shape[0] // group
    shape = (keys, group * keys)
    parts = [mm(picks(shape, 0, 1, g, group), merged) for g in range(group)]
    return jnp.concatenate(parts, axis=1).astype(BF16)


def merge_heads(wide, group):
    if group == 1:
        return wide
    keys = wide.shape[0]
    dim = wide.shape[1] // group
    shape = (group * keys, keys)
    parts = [
        mm(picks(shape, 1, 0, g, group), wide[:, g * dim : (g + 1) * dim]) for g in range(group)
    ]
    return sum(parts[1:], parts[0]).astype(BF16)


def kernel(
    n, heads, group,
    live_ref, q_ref, k_ref, v_ref, rk_ref, rv_ref, do_ref, seg_ref,
    out_ref, dq_ref, drk_ref, drv_ref, dpk_ref, dpv_ref,
    kv, q_t, do_t, q_w, do_w, w_all, w_loc, ds_low, mask_ref, o_acc, dq_acc,
    high, totals, delta_ref, loc_kv, v_turned, own_grad, hold,
    g_out, g_in, send_sem, recv_sem, gsend_sem, grecv_sem,
):
    merged = q_ref.shape[0]
    dim = q_ref.shape[1]
    keys = k_ref.shape[0] // group
    rkeys = rk_ref.shape[0] // group
    half = keys // 2
    width = 256
    chunks = merged // width
    scale = 1.0 / math.sqrt(dim)
    scale2 = scale * math.log2(math.e)
    me = lax.axis_index("blk")
    pair = n == 4
    if pair:
        xn = me + 1 - 2 * (me % 2)
        yn = (me + 2) % 4
        partners = [xn, yn]
    else:
        partners = [(me + s) % n for s in range(1, n)]

    barrier = pltpu.get_barrier_semaphore()
    for other in partners:
        pl.semaphore_signal(barrier, inc=1, device_id={"blk": other}, device_id_type=MESH)
    kv[0, 0] = split_heads(k_ref[...], group)
    kv[0, 1] = split_heads(v_ref[...], group)
    pl.semaphore_wait(barrier, len(partners))

    def move(src, dst, t, span, sem, other):
        return pltpu.make_async_remote_copy(
            src_ref=kv.at[src, t, span], dst_ref=kv.at[dst, t, span],
            send_sem=send_sem.at[sem], recv_sem=recv_sem.at[sem],
            device_id={"blk": other}, device_id_type=MESH,
        )

    low, upper, full = pl.ds(0, half), pl.ds(half, half), pl.ds(0, keys)
    gather = {}
    for t in range(2):
        if pair:
            gather[t, "lx"] = move(0, 1, t, low, 6 * t, xn)
            gather[t, "uy"] = move(0, 2, t, upper, 6 * t + 1, yn)
            gather[t, "ux"] = move(0, 1, t, upper, 6 * t + 2, xn)
            gather[t, "ly"] = move(0, 2, t, low, 6 * t + 3, yn)
            gather[t, "ld"] = move(1, 3, t, low, 6 * t + 4, yn)
            gather[t, "ud"] = move(2, 3, t, upper, 6 * t + 5, xn)
        else:
            for s in range(1, n):
                gather[t, s] = move(0, n - s, t, full, 2 * (n - s) + t, (me + s) % n)

    def begin(t):
        for name in ("lx", "uy", "ux", "ly") if pair else range(1, n):
            gather[t, name].start()

    def forward(t):
        if pair:
            gather[t, "lx"].wait_recv()
            gather[t, "ld"].start()
            gather[t, "uy"].wait_recv()
            gather[t, "ud"].start()

    def arrived(t, slot):
        if pair:
            for name in {1: ("ux",), 2: ("ly",), 3: ("ld", "ud")}[slot]:
                gather[t, name].wait_recv()
        else:
            gather[t, n - slot].wait_recv()

    begin(0)
    live = live_ref[0]

    def lanes(c):
        return pl.ds(pl.multiple_of(c * width, width), width)

    def loop(step, unroll):
        lax.fori_loop(0, chunks, lambda c, carry: step(c, lanes(c)), None, unroll=unroll)

    def prepare(c, at):
        row = lax.broadcasted_iota(jnp.int32, (width, dim), 0)
        owner = (row % heads) // (heads // group)
        alive = (row + c * width) // heads < live
        q = q_ref[at, :].astype(F32)
        do = jnp.where(alive, do_ref[at, :].astype(F32), 0.0)
        for value, wide, turned in ((q, q_w, q_t), (do, do_w, do_t)):
            for g in range(group):
                mine = jnp.where(owner == g, value, 0.0)
                span = slice(g * dim, (g + 1) * dim)
                wide[at, span] = mine.astype(BF16)
                turned[span, at] = mine.T.astype(BF16)

    loop(prepare, PREP_UNROLL)

    def own_head(wide):
        lane = lax.broadcasted_iota(jnp.int32, (dim, width), 1)
        owner = (lane % heads) // (heads // group)
        result = wide[:dim, :]
        for g in range(1, group):
            result = jnp.where(owner == g, wide[g * dim : (g + 1) * dim, :], result)
        return result

    def keys_of(s):
        return loc_kv[0] if s == n else kv[s, 0]

    def values_of(s):
        return loc_kv[1] if s == n else kv[s, 1]

    def weights_of(s):
        return w_loc if s == n else w_all.at[s]

    def exponentials(s):
        key = keys_of(s)
        store = weights_of(s)

        def step(c, at):
            score = mm(key, q_t[:, at])
            if s == n:
                score = jnp.where(mask_ref[:, at] > 0.5, score, -1e30)
            top = jnp.max(score, axis=0, keepdims=True)
            p = jnp.exp2((score - top) * scale2)
            store[:, at] = p.astype(BF16)
            high[s : s + 1, at] = top
            totals[s : s + 1, at] = jnp.sum(p, axis=0, keepdims=True)

        loop(step, UNROLL)

    exponentials(0)
    forward(0)
    begin(1)

    seg = seg_ref[...].astype(F32)
    ri = lax.broadcasted_iota(jnp.int32, (rkeys, rkeys), 0)
    ci = lax.broadcasted_iota(jnp.int32, (rkeys, rkeys), 1)
    seg_row = jnp.broadcast_to(seg, (rkeys, rkeys))
    seg_col = jnp.sum(jnp.where(ri == ci, seg_row, 0.0), axis=1, keepdims=True)
    allowed = jnp.where((ri <= ci) & (seg_col == seg_row), 1.0, 0.0).astype(BF16)
    er = lax.broadcasted_iota(jnp.int32, (rkeys, merged), 0)
    ec = lax.broadcasted_iota(jnp.int32, (rkeys, merged), 1)
    expand = (er == ec // heads).astype(F32).astype(BF16)
    mask_ref[...] = mm(allowed, expand)
    loc_kv[0] = split_heads(rk_ref[...], group)
    loc_kv[1] = split_heads(rv_ref[...], group)
    exponentials(n)
    for s in range(1, n):
        arrived(0, s)
        exponentials(s)

    def factors(c, at):
        tops = high[0 : n + 1, at]
        gain = jnp.exp2((tops - jnp.max(tops, axis=0, keepdims=True)) * scale2)
        total = jnp.sum(gain * totals[0 : n + 1, at], axis=0, keepdims=True)
        totals[0 : n + 1, at] = gain * (1.0 / total)

    loop(factors, PREP_UNROLL)

    def value_grad(s):
        store = weights_of(s)

        def step(c, at):
            w = store[:, at].astype(F32) * totals[s : s + 1, at]
            store[:, at] = w.astype(BF16)

        loop(step, UNROLL)
        return mm(store[...], do_w[...])

    def key_grad(s, first):
        key_t = keys_of(s).astype(F32).T.astype(BF16)
        value = values_of(s)
        store = weights_of(s)
        count = key_t.shape[1]

        def step(c, at):
            dprob = mm(value, do_t[:, at])
            ds = (store[:, at].astype(F32) * (dprob - delta_ref[0:1, at])).astype(BF16)
            ds_low[:count, at] = ds
            part = own_head(mm(key_t, ds))
            if first:
                dq_acc[:, at] = part
            else:
                dq_acc[:, at] += part

        loop(step, UNROLL)
        return mm(ds_low[:count, :], q_w[...]) * scale

    count = 6 if pair else n

    def give(t, slot, other):
        at = t * count + slot
        return pltpu.make_async_remote_copy(
            src_ref=g_out.at[at], dst_ref=g_in.at[at],
            send_sem=gsend_sem.at[at], recv_sem=grecv_sem.at[at],
            device_id={"blk": other}, device_id_type=MESH,
        )

    back = {}

    def send(t, slot, other, value):
        g_out[t * count + slot] = value.astype(BF16)
        back[t, slot] = give(t, slot, other)
        back[t, slot].start()

    def received(t, slot):
        back[t, slot].wait_recv()
        return g_in[t * count + slot].astype(F32)

    def direct(t, s, grad):
        if not pair:
            send(t, s, (me + s) % n, grad)
        elif s == 3:
            send(t, 0, xn, grad[:half])
            send(t, 1, yn, grad[half:])
        elif s == 1:
            send(t, 2, xn, grad[:half])
            hold[0] = grad[half:]
        else:
            send(t, 4, yn, grad[half:])
            hold[1] = grad[:half]

    def combined(t):
        if pair:
            send(t, 3, xn, hold[0] + received(t, 1))
            send(t, 5, yn, hold[1] + received(t, 0))

    def total_of(t, own):
        if pair:
            lower = own[:half] + received(t, 2) + received(t, 5)
            higher = own[half:] + received(t, 4) + received(t, 3)
            return jnp.concatenate([lower, higher], axis=0)
        for s in range(1, n):
            own = own + received(t, s)
        return own

    order = [3, 1, 2] if pair else list(range(1, n))
    for s in order:
        direct_grad = value_grad(s)
        if s == order[0]:
            forward(1)
        direct(0, s, direct_grad)
    drv_ref[...] = merge_heads(value_grad(n).astype(BF16), group)
    own_grad[...] = value_grad(0)

    def turn_values(s):
        value_t = values_of(s).astype(F32).T.astype(BF16)
        if s == n:
            v_turned[n, :, :rkeys] = value_t
        else:
            v_turned[s] = value_t

    def output_part(slots, at):
        total = None
        for s in slots:
            turned = v_turned[n, :, :rkeys] if s == n else v_turned[s]
            part = mm(turned, weights_of(s)[:, at])
            total = part if total is None else total + part
        return own_head(total)

    early = [0, n, 1, 2] if pair else [0, n]
    late = [3] if pair else list(range(1, n))
    for s in early:
        if 0 < s < n:
            arrived(1, s)
        turn_values(s)

    def begin_output(c, at):
        o_acc[:, at] = output_part(early, at)

    loop(begin_output, PREP_UNROLL)
    for s in late:
        arrived(1, s)
        turn_values(s)

    def finish(c, at):
        lane = lax.broadcasted_iota(jnp.int32, (1, width), 1) + c * width
        alive = (lane // heads) < live
        o = o_acc[:, at] + output_part(late, at)
        o = jnp.where(alive, o, 0.0).astype(BF16).astype(F32)
        out_ref[at, :] = o.T.astype(BF16)
        do = own_head(do_t[:, at].astype(F32))
        delta_ref[0:1, at] = jnp.sum(do * o, axis=0, keepdims=True)

    loop(finish, PREP_UNROLL)
    combined(0)
    for s in order:
        direct(1, s, key_grad(s, s == order[0]))
    drk_ref[...] = merge_heads(key_grad(n, False).astype(BF16), group)
    combined(1)
    own_key = key_grad(0, False)

    def last(c, at):
        dq_ref[at, :] = (dq_acc[:, at] * scale).T.astype(BF16)

    loop(last, PREP_UNROLL)
    dpv_ref[...] = merge_heads(total_of(0, own_grad[...]).astype(BF16), group)
    dpk_ref[...] = merge_heads(total_of(1, own_key).astype(BF16), group)
    for copy in list(gather.values()) + list(back.values()):
        copy.wait_send()


def store_kernel(*refs):
    count = len(refs) // 2
    for i in range(count):
        refs[count + i][...] = refs[i][...]


def store(results):
    vmem = pl.BlockSpec(memory_space=pltpu.VMEM)
    return pl.pallas_call(
        store_kernel,
        out_shape=[jax.ShapeDtypeStruct(r.shape, r.dtype) for r in results],
        in_specs=[vmem] * len(results),
        out_specs=[vmem] * len(results),
    )(*results)


def on_device(n, resp_q, prompt_k, prompt_v, resp_k, resp_v, d_out, segment_ids, live_rows):
    rows, heads, dim = resp_q.shape
    keys, kvh, _ = prompt_k.shape
    rkeys = resp_k.shape[0]
    merged = rows * heads
    flat = lambda a: a.reshape(-1, dim)
    vmem = pl.BlockSpec(memory_space=pltpu.VMEM)
    stats = ((n + 2 + 7) // 8) * 8
    grads = (12, keys // 2, kvh * dim) if n == 4 else (2 * n, keys, kvh * dim)
    results = pl.pallas_call(
        functools.partial(kernel, n, heads, kvh),
        out_shape=[
            jax.ShapeDtypeStruct((merged, dim), BF16),
            jax.ShapeDtypeStruct((merged, dim), BF16),
            jax.ShapeDtypeStruct((rkeys * kvh, dim), BF16),
            jax.ShapeDtypeStruct((rkeys * kvh, dim), BF16),
            jax.ShapeDtypeStruct((keys * kvh, dim), BF16),
            jax.ShapeDtypeStruct((keys * kvh, dim), BF16),
        ],
        in_specs=[pl.BlockSpec(memory_space=pltpu.SMEM)] + [vmem] * 7,
        out_specs=[vmem] * 6,
        scratch_shapes=[
            pltpu.VMEM((n, 2, keys, kvh * dim), BF16),
            pltpu.VMEM((kvh * dim, merged), BF16),
            pltpu.VMEM((kvh * dim, merged), BF16),
            pltpu.VMEM((merged, kvh * dim), BF16),
            pltpu.VMEM((merged, kvh * dim), BF16),
            pltpu.VMEM((n, keys, merged), BF16),
            pltpu.VMEM((rkeys, merged), BF16),
            pltpu.VMEM((keys, merged), BF16),
            pltpu.VMEM((rkeys, merged), F32),
            pltpu.VMEM((dim, merged), F32),
            pltpu.VMEM((dim, merged), F32),
            pltpu.VMEM((stats, merged), F32),
            pltpu.VMEM((stats, merged), F32),
            pltpu.VMEM((8, merged), F32),
            pltpu.VMEM((2, rkeys, kvh * dim), BF16),
            pltpu.VMEM((n + 1, kvh * dim, keys), BF16),
            pltpu.VMEM((keys, kvh * dim), F32),
            pltpu.VMEM((2, keys // 2, kvh * dim), F32),
            pltpu.VMEM(grads, BF16),
            pltpu.VMEM(grads, BF16),
            pltpu.SemaphoreType.DMA((max(12, 2 * n),)),
            pltpu.SemaphoreType.DMA((max(12, 2 * n),)),
            pltpu.SemaphoreType.DMA((grads[0],)),
            pltpu.SemaphoreType.DMA((grads[0],)),
        ],
        compiler_params=pltpu.CompilerParams(
            collective_id=0, has_side_effects=True, vmem_limit_bytes=60 * 1024 * 1024
        ),
        cost_estimate=pl.CostEstimate(
            flops=12 * merged * dim * (n * keys + rkeys),
            bytes_accessed=4 * merged * dim * 2,
            transcendentals=merged * (n * keys + rkeys),
        ),
    )(
        live_rows, flat(resp_q), flat(prompt_k), flat(prompt_v), flat(resp_k), flat(resp_v),
        flat(d_out), segment_ids,
    )
    results = store(results)
    shapes = (resp_q, resp_q, resp_k, resp_v, prompt_k, prompt_v)
    return tuple(r.reshape(s.shape) for r, s in zip(results, shapes))


def solution(mesh):
    split = P(("group", "blk"), "kvh", None)
    return jax.shard_map(
        functools.partial(on_device, mesh.shape["blk"]),
        mesh=mesh,
        in_specs=(split,) * 6 + (P(("group", "blk"), None), P(("group", "blk"))),
        out_specs=(split,) * 6,
        check_vma=False,
    )
```
